512 devices in a mesh: chan: 16 (over z_lo, core), tok: 32 (over z_hi, y, x).
Axes of the slice: x: 4, y: 4, z: 16 (z_hi: 2, z_lo: 8; z = z_hi * 8 + z_lo), core: 2. Of those that a mesh axis runs over, the one named last changes fastest.
Arguments:
- codes: bfloat16 [38400, 16384], P('tok', 'chan'), may hold values from -6 to 6
- scale_exp: int32 [16384], P('chan'), may hold values from -2 to 2
- delta: bfloat16 [38400, 16384], P('tok', 'chan'), may hold values from -4 to 4
Outputs:
- gram: float32 [16384, 512], P(('chan', 'tok'))
- mismatch: float32 [16384, 512], P(('chan', 'tok'))
The draws below stay inside these ranges and needn't reach their ends.
All inputs are finite; a program needn't handle non-finite values.
Results may differ from the reference program's by a relative error of at most 0.0003.
Values may be sent and summed in bfloat16 or wider, within the bound.
A program may use at most 64 MiB of HBM per device.

```python
import jax
import jax.numpy as jnp

C = 16384
WCOL = 32
TOKENS = 38400
N_CHAN = 16


def set_ends(drawn, stream_key, smallest, largest):
    longest = drawn.shape.index(max(drawn.shape))
    spots = []
    for shift in (0, 1):
        where = [jax.random.randint(jax.random.fold_in(stream_key, axis), (), 0, length) for axis, length in enumerate(drawn.shape)]
        where[longest] = (where[longest] + shift) % drawn.shape[longest]
        spots.append(tuple(where))
    return drawn.at[spots[0]].set(smallest).at[spots[1]].set(largest)


def shard_levels(stream_key, shape, cuts, least, top_value):
    loudness, own = 1.0, jax.random.fold_in(stream_key, 6)
    for dim, blocks in cuts:
        steps = jnp.exp(jax.random.uniform(jax.random.fold_in(own, dim), (blocks,), jnp.float32, least / len(cuts), top_value / len(cuts)))
        loudness = loudness * jnp.repeat(steps, shape[dim] // blocks).reshape([-1 if axis == dim else 1 for axis in range(len(shape))])
    return loudness


def bell_draw(own_key, dims, deviation, limit, shards=(), kind=jnp.bfloat16):
    factor_of = shard_levels(own_key, dims, shards, -0.22, 0.18) if shards else 1.0
    values = jax.random.normal(own_key, dims, jnp.float32) * deviation * factor_of
    return jnp.minimum(jnp.maximum(values, -limit), limit).astype(kind)


def setup_inputs(seed: int = 0) -> dict:
    keys = jax.random.split(jax.random.key(seed), 4)
    return {
        "codes": bell_draw(keys[0], (TOKENS, C), 1.0, 6.0, ((0, 32), (1, 16))),
        "scale_exp": set_ends(jax.random.randint(keys[1], (C,), -2, 3), jax.random.fold_in(keys[1], 1), -2, 2).astype(jnp.int32),
        "delta": bell_draw(keys[2], (TOKENS, C), 0.5, 4.0, ((0, 32), (1, 16))),
    }


def reference(codes, scale_exp, delta):
    scale = jnp.exp2(scale_exp.astype(jnp.float32)).astype(jnp.bfloat16)
    xq = codes * scale[None, :]
    rows = xq.shape[0]
    win = xq.reshape(rows, N_CHAN, C // N_CHAN)[:, :, :WCOL].reshape(rows, WCOL * N_CHAN)
    gram = jnp.dot(xq.T, win, preferred_element_type=jnp.float32) / jnp.float32(TOKENS)
    mismatch = jnp.dot(delta.T, win, preferred_element_type=jnp.float32) / jnp.sqrt(jnp.float32(TOKENS))
    return (gram, mismatch)
```

```python
import functools

import jax
import jax.numpy as jnp
from jax import lax
from jax.experimental import pallas as pl
from jax.experimental.pallas import tpu as pltpu
from jax.sharding import Mesh
from jax.sharding import PartitionSpec as P

WCOL = 32
AXES = ("zlo", "core", "zhi", "y", "x")
TOK = ("zhi", "y", "x")
MESH = pl.DeviceIdType.MESH
F32, BF16, I32, I16 = jnp.float32, jnp.bfloat16, jnp.int32, jnp.int16

DIRECT = {
    0: (1, 4), 1: (0, 2, 5), 2: (1, 3, 6), 3: (2, 4, 1, 6),
    4: (3, 1, 6), 5: (4, 1, 6), 6: (5, 7, 2), 7: (6, 3),
}
RELAY = {
    0: {},
    1: {0: (2,), 2: (0,), 3: (0,), 4: (0, 2), 5: (0, 2)},
    2: {1: (3,), 6: (0, 1, 3)},
    3: {2: (4,), 7: (0, 1, 2, 4)},
    4: {0: (3, 5, 6, 7), 3: (5,), 5: (3,)},
    5: {1: (4, 6, 7), 6: (4,)},
    6: {2: (5, 7), 3: (7,), 4: (5, 7), 5: (7,), 7: (5,)},
    7: {},
}
TAKE = {
    0: (1, 2, 3, 4, 5, 6, 7), 1: (2, 0, 3, 4, 5, 6, 7), 2: (3, 1, 6, 0, 7, 4, 5), 3: (2, 4, 7, 5, 6, 1, 0),
    4: (5, 3, 0, 2, 1, 6, 7), 5: (4, 6, 1, 7, 3, 2, 0), 6: (7, 5, 4, 3, 2, 0, 1), 7: (6, 5, 4, 3, 2, 1, 0),
}
CHUNKS = {
    0: (0, 1, 2, 3), 1: (0, 1, 2, 3), 2: (1, 0, 3, 2), 3: (1, 2, 3, 0),
    4: (2, 1, 0, 3), 5: (2, 3, 1, 0), 6: (3, 2, 1, 0), 7: (3, 2, 1, 0),
}
STEPS = ((0, 1), (2, 3), (4, 5), (6,))
TOP = 32000.0


def coded(value, groups):
    blocks = value.reshape(groups, 32, 128)
    largest = jnp.maximum(jnp.max(jnp.abs(blocks), axis=1), 2.0**-110)
    eighths = jnp.ceil(jnp.log2(largest) * 8.0)
    factor = jnp.exp2(eighths * -0.125) * TOP
    whole = jnp.round(blocks * factor[:, None, :]).astype(I32).astype(I16)
    if groups < 16:
        eighths = jnp.concatenate([eighths, jnp.zeros((16 - groups, 128), F32)], axis=0)
    return whole.reshape(groups * 32, 128), eighths.astype(I32).astype(I16)


def decoded(ref, at, groups):
    rows = groups * 32
    whole = ref[(*at, pl.ds(0, rows), slice(None))].astype(I32).astype(F32)
    eighths = ref[(*at, pl.ds(rows, 16), slice(None))].astype(I32).astype(F32)[:groups]
    factor = jnp.exp2(eighths * 0.125) * (1.0 / TOP)
    return (whole.reshape(groups, 32, 128) * factor[:, None, :]).reshape(rows, 128)


def kernel(total, codes, scale_exp, delta, gram, mismatch, xs, ds, scale, left, win, own1, own2,
           s1, r1, s2, r2, s3, r3, load_sem, wsend, wrecv, csend, crecv, q1s, q1r, q2s, q2r, q3s, q3r, go_sem):
    tokens, width = codes.shape
    padded = xs.shape[0]
    zlo, core, zhi, y, x = (lax.axis_index(a) for a in AXES)
    z = zhi * 8 + zlo

    def along(d):
        n = lax.rem(z + (d + 16), 16)
        return {"zhi": n // 8, "zlo": lax.rem(n, 8)}

    loads = [
        pltpu.make_async_copy(codes.at[:, pl.ds(0, 128)], xs.at[pl.ds(0, tokens), pl.ds(0, 128)], load_sem.at[0]),
        pltpu.make_async_copy(scale_exp, scale, load_sem.at[1]),
        pltpu.make_async_copy(codes.at[:, pl.ds(128, width - 128)], xs.at[pl.ds(0, tokens), pl.ds(128, width - 128)], load_sem.at[2]),
        pltpu.make_async_copy(delta, ds.at[pl.ds(0, tokens)], load_sem.at[3]),
    ]
    for c in loads:
        c.start()
    barrier = pltpu.get_barrier_semaphore()
    greet = [{"core": 1 - core}]
    greet += [along(d) for d in (1, -1, 2, -2, 3, -3, 4, -4)]
    greet += [{a: lax.rem(lax.axis_index(a) + k, 4)} for a in ("x", "y") for k in (1, 2, 3)]
    for who in greet:
        pl.semaphore_signal(barrier, inc=1, device_id=who, device_id_type=MESH)

    xs[pl.ds(tokens, padded - tokens), :] = jnp.zeros((padded - tokens, width), BF16)
    ds[pl.ds(tokens, padded - tokens), :] = jnp.zeros((padded - tokens, width), BF16)
    loads[0].wait()
    loads[1].wait()

    def factors(i):
        return jnp.exp2(scale[pl.ds(i, 1), :].astype(F32)).astype(BF16)

    my_rows = pl.ds(pl.multiple_of((zlo * 2 + core) * WCOL, WCOL), WCOL)
    win[my_rows, :] = (xs[:, pl.ds(0, 128)] * factors(0)).T[:WCOL]

    loads[2].wait()
    loads[3].wait()

    def place(i, stat, block):
        hi, row = i // 4, lax.rem(i, 4)
        for k in range(4):
            first = jnp.where(hi == 0, k * 4 + row, row * 4 + k)
            start = pl.multiple_of(hi * width + (first * 2 + stat) * 32, 32)
            left[pl.ds(start, 32), :] = block[k * 32 : (k + 1) * 32]

    @pl.loop(0, width // 128)
    def _(i):
        lanes = pl.ds(pl.multiple_of(i * 128, 128), 128)
        place(i, 0, (xs[:, lanes] * factors(i)).T)
        place(i, 1, ds[:, lanes].T)

    pl.semaphore_wait(barrier, len(greet))
    pl.semaphore_signal(go_sem, inc=1, device_id=along(4), device_id_type=MESH)

    def block_rows(s, c):
        return pl.ds(pl.multiple_of((s * 2 + c) * WCOL, WCOL), WCOL)

    def hand(s, to):
        return pltpu.make_async_remote_copy(
            src_ref=win.at[block_rows(s, core)], dst_ref=win.at[block_rows(s, core)],
            send_sem=wsend.at[s, to], recv_sem=wrecv.at[s],
            device_id={"zlo": to}, device_id_type=MESH)

    def across(s):
        return pltpu.make_async_remote_copy(
            src_ref=win.at[block_rows(s, core)], dst_ref=win.at[block_rows(s, core)],
            send_sem=csend.at[s], recv_sem=crecv.at[s],
            device_id={"core": 1 - core}, device_id_type=MESH)

    def sent_by(a):
        return [(a, to) for to in DIRECT[a]] + [(s, to) for s, tos in RELAY[a].items() for to in tos]

    across(zlo).start()
    for a in range(8):
        @pl.when(zlo == a)
        def _(a=a):
            for to in DIRECT[a]:
                hand(a, to).start()

    def take(a, n):
        s = TAKE[a][n]
        hand(s, a).wait_recv()
        for to in RELAY[a].get(s, ()):
            hand(s, to).start()
        across(s).start()

    def taken(a, n):
        across(TAKE[a][n]).wait_recv()

    def chunk_of(k):
        q = jnp.int32(0)
        for a in range(8):
            for n in range(4):
                q = jnp.where((zlo == a) & (k == n), CHUNKS[a][n], q)
        return q

    axes = (("x", "y"), ("y", "x"))

    def send1(k, h, j):
        to = lax.rem(lax.axis_index(axes[h][0]) + j + 1, 4)
        return pltpu.make_async_remote_copy(
            src_ref=s1.at[k, h, j], dst_ref=r1.at[k, h, j], send_sem=q1s.at[k, h, j], recv_sem=q1r.at[k, h, j],
            device_id={axes[h][0]: to}, device_id_type=MESH)

    def send2(k, h, j):
        to = lax.rem(lax.axis_index(axes[h][1]) + j + 1, 4)
        return pltpu.make_async_remote_copy(
            src_ref=s2.at[k, h, j], dst_ref=r2.at[k, h, j], send_sem=q2s.at[k, h, j], recv_sem=q2r.at[k, h, j],
            device_id={axes[h][1]: to}, device_id_type=MESH)

    def send3(k):
        return pltpu.make_async_remote_copy(
            src_ref=s3.at[k], dst_ref=r3.at[k], send_sem=q3s.at[k], recv_sem=q3r.at[k],
            device_id={"zhi": 1 - zhi}, device_id_type=MESH)

    def multiply(k):
        q = chunk_of(k)
        right = win[pl.ds(pl.multiple_of(q * 128, 128), 128), :]

        def tile(h, t):
            rows = pl.ds(pl.multiple_of(h * width + t * 256, 256), 256)
            return lax.dot_general(left[rows, :], right, (((1,), (1,)), ((), ())), preferred_element_type=F32)

        for h in range(2):
            me = lax.axis_index(axes[h][0])

            @pl.loop(0, 3)
            def _(j, h=h, me=me):
                whole, eighths = coded(tile(h, lax.rem(me + j + 1, 4)), 8)
                s1[k, h, j, pl.ds(0, 256), :] = whole
                s1[k, h, j, pl.ds(256, 16), :] = eighths
                send1(k, h, j).start()

            own1[k, h] = tile(h, me)

    def second(k):
        for h in range(2):
            for j in range(3):
                send1(k, h, j).wait_recv()
            me = lax.axis_index(axes[h][1])
            own1[k, h] = own1[k, h] + decoded(r1, (k, h, 0), 8) + decoded(r1, (k, h, 1), 8) + decoded(r1, (k, h, 2), 8)
            for j in range(3):
                t = lax.rem(me + j + 1, 4)
                whole, eighths = coded(own1[k, h, pl.ds(pl.multiple_of(t * 64, 64), 64), :], 2)
                s2[k, h, j, pl.ds(0, 64), :] = whole
                s2[k, h, j, pl.ds(64, 16), :] = eighths
                send2(k, h, j).start()
            own2[k, h] = own1[k, h, pl.ds(pl.multiple_of(me * 64, 64), 64), :]

    def third(k):
        for h in range(2):
            for j in range(3):
                send2(k, h, j).wait_recv()
            own2[k, h] = own2[k, h] + decoded(r2, (k, h, 0), 2) + decoded(r2, (k, h, 1), 2) + decoded(r2, (k, h, 2), 2)
        whole, eighths = coded(own2[k, 1 - zhi], 2)
        s3[k, pl.ds(0, 64), :] = whole
        s3[k, pl.ds(64, 16), :] = eighths
        send3(k).start()

    def last(k):
        send3(k).wait_recv()
        result = own2[k, zhi] + decoded(r3, (k,), 2)
        lanes = pl.ds(pl.multiple_of(chunk_of(k) * 128, 128), 128)
        gram[:, lanes] = result[:32] * (1.0 / total)
        mismatch[:, lanes] = result[32:] * (1.0 / total**0.5)

    @pl.loop(0, 7)
    def _(phase):
        for n in range(4):
            for a in range(8):
                @pl.when((phase == n) & (zlo == a))
                def _(n=n, a=a):
                    for e in STEPS[n]:
                        take(a, e)
                    if n == 0:
                        across(a).wait_recv()
                    for e in STEPS[n]:
                        taken(a, e)

        @pl.when(phase < 4)
        def _():
            multiply(phase)

        @pl.when((phase >= 1) & (phase < 5))
        def _():
            second(phase - 1)

        @pl.when(phase == 2)
        def _():
            pl.semaphore_wait(go_sem, 1)

        @pl.when((phase >= 2) & (phase < 6))
        def _():
            third(phase - 2)

        @pl.when(phase >= 3)
        def _():
            last(phase - 3)

    for a in range(8):
        @pl.when(zlo == a)
        def _(a=a):
            for s, to in sent_by(a):
                hand(s, to).wait_send()

    @pl.loop(0, 8)
    def _(s):
        across(s).wait_send()

    @pl.loop(0, 4)
    def _(k):
        for h in range(2):
            for j in range(3):
                send1(k, h, j).wait_send()
                send2(k, h, j).wait_send()
        send3(k).wait_send()


def shards(codes, scale_exp, delta):
    tokens, width = codes.shape
    total = float(tokens * lax.axis_size(TOK))
    padded = -(-tokens // 128) * 128
    dma = pltpu.SemaphoreType.DMA
    return pl.pallas_call(
        functools.partial(kernel, total),
        out_shape=(jax.ShapeDtypeStruct((32, 512), F32), jax.ShapeDtypeStruct((32, 512), F32)),
        in_specs=[pl.BlockSpec(memory_space=pl.ANY)] * 3,
        out_specs=(pl.BlockSpec(memory_space=pltpu.VMEM),) * 2,
        scratch_shapes=[
            pltpu.VMEM((padded, width), BF16),
            pltpu.VMEM((padded, width), BF16),
            pltpu.VMEM((8, 128), I32),
            pltpu.VMEM((2 * width, padded), BF16),
            pltpu.VMEM((512, padded), BF16),
            pltpu.VMEM((4, 2, 256, 128), F32),
            pltpu.VMEM((4, 2, 64, 128), F32),
            pltpu.VMEM((4, 2, 3, 272, 128), I16),
            pltpu.VMEM((4, 2, 3, 272, 128), I16),
            pltpu.VMEM((4, 2, 3, 80, 128), I16),
            pltpu.VMEM((4, 2, 3, 80, 128), I16),
            pltpu.VMEM((4, 80, 128), I16),
            pltpu.VMEM((4, 80, 128), I16),
            dma((4,)),
            dma((8, 8)),
            dma((8,)),
            dma((8,)),
            dma((8,)),
            dma((4, 2, 3)),
            dma((4, 2, 3)),
            dma((4, 2, 3)),
            dma((4, 2, 3)),
            dma((4,)),
            dma((4,)),
            pltpu.SemaphoreType.REGULAR,
        ],
        compiler_params=pltpu.CompilerParams(
            collective_id=0, has_side_effects=True, vmem_limit_bytes=56 * 2**20
        ),
        cost_estimate=pl.CostEstimate(
            flops=2 * 2 * width * 512 * tokens, bytes_accessed=4 * tokens * width, transcendentals=0
        ),
    )(codes, scale_exp.reshape(width // 128, 128), delta)


def solution(mesh):
    split = Mesh(mesh.devices.reshape(8, 2, 2, 4, 4), AXES)
    chan = ("zlo", "core")
    return jax.shard_map(
        shards,
        mesh=split,
        in_specs=(P(TOK, chan), P(chan), P(TOK, chan)),
        out_specs=(P((*chan, *TOK), None), P((*chan, *TOK), None)),
        check_vma=False,
    )
```

```python
import functools

import jax
import jax.numpy as jnp
from jax import lax
from jax.experimental import pallas as pl
from jax.experimental.pallas import tpu as pltpu
from jax.sharding import Mesh
from jax.sharding import PartitionSpec as P

WCOL = 32
AXES = ("zlo", "core", "zhi", "y", "x")
TOK = ("zhi", "y", "x")
MESH = pl.DeviceIdType.MESH
F32, BF16, I32, I16 = jnp.float32, jnp.bfloat16, jnp.int32, jnp.int16

DIRECT = {
    0: (4, 1),
    1: (5, 2, 0),
    2: (6, 1, 3),
    3: (6, 1, 4, 2),
    4: (1, 6, 3),
    5: (1, 4, 6),
    6: (2, 5, 7),
    7: (3, 6),
}
RELAY = {
    0: {},
    1: {0: (2,), 2: (0,), 3: (0,), 4: (0, 2), 5: (0, 2)},
    2: {1: (3,), 6: (0, 1, 3)},
    3: {2: (4,), 7: (0, 1, 2, 4)},
    4: {3: (5,), 5: (3,), 0: (7, 6, 3, 5)},
    5: {6: (4,), 1: (7, 4, 6)},
    6: {5: (7,), 7: (5,), 4: (5, 7), 3: (7,), 2: (5, 7)},
    7: {},
}
CHUNKS = {
    0: (0, 1, 2, 3),
    1: (0, 1, 2, 3),
    2: (1, 0, 2, 3),
    3: (1, 2, 0, 3),
    4: (2, 1, 3, 0),
    5: (2, 3, 1, 0),
    6: (3, 2, 1, 0),
    7: (3, 2, 1, 0),
}
PARTS = 5
TOP = 32000.0


def coded(value, groups):
    blocks = value.reshape(groups, 32, 128)
    largest = jnp.maximum(jnp.max(jnp.abs(blocks), axis=1), 2.0**-110)
    eighths = jnp.ceil(jnp.log2(largest) * 8.0)
    factor = jnp.exp2(eighths * -0.125) * TOP
    whole = jnp.round(blocks * factor[:, None, :]).astype(I32).astype(I16)
    if groups < 16:
        eighths = jnp.concatenate([eighths, jnp.zeros((16 - groups, 128), F32)], axis=0)
    return whole.reshape(groups * 32, 128), eighths.astype(I32).astype(I16)


def decoded(ref, at, groups):
    rows = groups * 32
    whole = ref[(*at, pl.ds(0, rows), slice(None))].astype(I32).astype(F32)
    eighths = ref[(*at, pl.ds(rows, 16), slice(None))].astype(I32).astype(F32)[:groups]
    factor = jnp.exp2(eighths * 0.125) * (1.0 / TOP)
    return (whole.reshape(groups, 32, 128) * factor[:, None, :]).reshape(rows, 128)


def kernel(total, codes, scale_exp, delta, out, xs, ds, scale, left, win, product, own1, own2,
           s1, r1, s2, r2, s3, r3, load_sem, wsend, wrecv, wpart, csend, crecv, q1s, q1r, q2s, q2r, q3s, q3r, go_sem):
    tokens, width = codes.shape
    padded = xs.shape[0]
    zlo, core, zhi, y, x = (lax.axis_index(a) for a in AXES)
    z = zhi * 8 + zlo

    def along(d):
        n = lax.rem(z + (d + 16), 16)
        return {"zhi": n // 8, "zlo": lax.rem(n, 8)}

    loads = [
        pltpu.make_async_copy(codes.at[:, pl.ds(0, 128)], xs.at[pl.ds(0, tokens), pl.ds(0, 128)], load_sem.at[0]),
        pltpu.make_async_copy(scale_exp, scale, load_sem.at[1]),
        pltpu.make_async_copy(codes.at[:, pl.ds(128, width - 128)], xs.at[pl.ds(0, tokens), pl.ds(128, width - 128)], load_sem.at[2]),
        pltpu.make_async_copy(delta, ds.at[pl.ds(0, tokens)], load_sem.at[3]),
    ]
    for c in loads:
        c.start()
    barrier = pltpu.get_barrier_semaphore()
    greet = [{"core": 1 - core}]
    greet += [along(d) for d in (1, -1, 2, -2, 3, -3, 4, -4)]
    greet += [{a: lax.rem(lax.axis_index(a) + k, 4)} for a in ("x", "y") for k in (1, 2, 3)]
    for who in greet:
        pl.semaphore_signal(barrier, inc=1, device_id=who, device_id_type=MESH)

    xs[pl.ds(tokens, padded - tokens), :] = jnp.zeros((padded - tokens, width), BF16)
    ds[pl.ds(tokens, padded - tokens), :] = jnp.zeros((padded - tokens, width), BF16)
    loads[0].wait()
    loads[1].wait()

    def factors(i):
        return jnp.exp2(scale[pl.ds(i, 1), :].astype(F32)).astype(BF16)

    my_rows = pl.ds(pl.multiple_of((zlo * 2 + core) * WCOL, WCOL), WCOL)
    win[my_rows, :] = (xs[:, pl.ds(0, 128)] * factors(0)).T[:WCOL]

    def place(i, stat, block):
        hi, row = i // 4, lax.rem(i, 4)
        for k in range(4):
            first = jnp.where(hi == 0, k * 4 + row, row * 4 + k)
            start = pl.multiple_of(hi * width + (first * 2 + stat) * 32, 32)
            left[pl.ds(start, 32), :] = block[k * 32 : (k + 1) * 32]

    pl.semaphore_wait(barrier, len(greet))
    pl.semaphore_signal(go_sem, inc=1, device_id=along(4), device_id_type=MESH)

    def block_rows(s, c):
        return pl.ds(pl.multiple_of((s * 2 + c) * WCOL, WCOL), WCOL)

    def hand(s, to, part=None, recv=None):
        size = padded // PARTS
        lanes = pl.ds(0, padded) if part is None else pl.ds(part * size, size)
        block = win.at[block_rows(s, core), lanes]
        return pltpu.make_async_remote_copy(
            src_ref=block, dst_ref=block, send_sem=wsend.at[s, to], recv_sem=wrecv.at[s] if recv is None else recv,
            device_id={"zlo": to}, device_id_type=MESH)

    def across(s):
        return pltpu.make_async_remote_copy(
            src_ref=win.at[block_rows(s, core)], dst_ref=win.at[block_rows(s, core)],
            send_sem=csend.at[s], recv_sem=crecv.at[s],
            device_id={"core": 1 - core}, device_id_type=MESH)

    def sent_by(a):
        return [(a, to) for to in DIRECT[a]] + [(s, to) for s, tos in RELAY[a].items() for to in tos]

    across(zlo).start()
    for a in range(8):
        @pl.when(zlo == a)
        def _(a=a):
            for part in range(PARTS):
                for to in DIRECT[a]:
                    if a in RELAY[to]:
                        hand(a, to, part, wpart.at[a, part]).start()
            for to in DIRECT[a]:
                if a not in RELAY[to]:
                    hand(a, to).start()
            pass

    loads[2].wait()
    loads[3].wait()

    @pl.loop(0, width // 128)
    def _(i):
        lanes = pl.ds(pl.multiple_of(i * 128, 128), 128)
        place(i, 0, (xs[:, lanes] * factors(i)).T)
        place(i, 1, ds[:, lanes].T)

    for a in range(8):
        @pl.when(zlo == a)
        def _(a=a):
            for s, tos in RELAY[a].items():
                for part in range(PARTS):
                    hand(s, a, part, wpart.at[s, part]).wait_recv()
                    for to in tos:
                        hand(s, to, part).start()
                across(s).start()

    def take(a, n):
        pair = (2 * CHUNKS[a][n], 2 * CHUNKS[a][n] + 1)
        for s in pair:
            if s != a and s not in RELAY[a]:
                hand(s, a).wait_recv()
                across(s).start()
        for s in pair:
            across(s).wait_recv()

    def chunk_of(k):
        q = jnp.int32(0)
        for a in range(8):
            for n in range(4):
                q = jnp.where((zlo == a) & (k == n), CHUNKS[a][n], q)
        return q

    axes = (("x", "y"), ("y", "x"))

    def send1(k, h, j):
        to = lax.rem(lax.axis_index(axes[h][0]) + j + 1, 4)
        return pltpu.make_async_remote_copy(
            src_ref=s1.at[k, h, j], dst_ref=r1.at[k, h, j], send_sem=q1s.at[k, h, j], recv_sem=q1r.at[k, h, j],
            device_id={axes[h][0]: to}, device_id_type=MESH)

    def send2(k, h, j):
        to = lax.rem(lax.axis_index(axes[h][1]) + j + 1, 4)
        return pltpu.make_async_remote_copy(
            src_ref=s2.at[k, h, j], dst_ref=r2.at[k, h, j], send_sem=q2s.at[k, h, j], recv_sem=q2r.at[k, h, j],
            device_id={axes[h][1]: to}, device_id_type=MESH)

    def send3(k):
        return pltpu.make_async_remote_copy(
            src_ref=s3.at[k], dst_ref=r3.at[k], send_sem=q3s.at[k], recv_sem=q3r.at[k],
            device_id={"zhi": 1 - zhi}, device_id_type=MESH)

    def multiply(k):
        q = chunk_of(k)
        right = win[pl.ds(pl.multiple_of(q * 128, 128), 128), :]

        for h in range(2):
            me = lax.axis_index(axes[h][0])
            product[h] = lax.dot_general(
                left[pl.ds(h * width, width), :], right, (((1,), (1,)), ((), ())), preferred_element_type=F32
            ).reshape(4, width // 4, 128)

            @pl.loop(0, 3)
            def _(j, h=h, me=me):
                whole, eighths = coded(product[h, lax.rem(me + j + 1, 4)], 8)
                s1[k, h, j, pl.ds(0, 256), :] = whole
                s1[k, h, j, pl.ds(256, 16), :] = eighths
                send1(k, h, j).start()

            own1[k, h] = product[h, me]

    def second(k):
        for h in range(2):
            for j in range(3):
                send1(k, h, j).wait_recv()
            me = lax.axis_index(axes[h][1])
            own1[k, h] = own1[k, h] + decoded(r1, (k, h, 0), 8) + decoded(r1, (k, h, 1), 8) + decoded(r1, (k, h, 2), 8)
            for j in range(3):
                t = lax.rem(me + j + 1, 4)
                whole, eighths = coded(own1[k, h, pl.ds(pl.multiple_of(t * 64, 64), 64), :], 2)
                s2[k, h, j, pl.ds(0, 64), :] = whole
                s2[k, h, j, pl.ds(64, 16), :] = eighths
                send2(k, h, j).start()
            own2[k, h] = own1[k, h, pl.ds(pl.multiple_of(me * 64, 64), 64), :]

    def third(k):
        for h in range(2):
            for j in range(3):
                send2(k, h, j).wait_recv()
            own2[k, h] = own2[k, h] + decoded(r2, (k, h, 0), 2) + decoded(r2, (k, h, 1), 2) + decoded(r2, (k, h, 2), 2)
        whole, eighths = coded(own2[k, 1 - zhi], 2)
        s3[k, pl.ds(0, 64), :] = whole
        s3[k, pl.ds(64, 16), :] = eighths
        send3(k).start()

    def last(k):
        send3(k).wait_recv()
        result = own2[k, zhi] + decoded(r3, (k,), 2)
        lanes = pl.ds(pl.multiple_of(chunk_of(k) * 128, 128), 128)
        out[:, lanes] = result

    @pl.loop(0, 4)
    def _(phase):
        for n in range(4):
            for a in range(8):
                @pl.when((phase == n) & (zlo == a))
                def _(n=n, a=a):
                    take(a, n)

        multiply(phase)

        @pl.when(phase >= 1)
        def _():
            second(phase - 1)

        @pl.when(phase == 2)
        def _():
            pl.semaphore_wait(go_sem, 1)

        @pl.when(phase >= 2)
        def _():
            third(phase - 2)

    second(3)
    third(2)
    third(3)

    @pl.loop(0, 4)
    def _(k):
        last(k)

    for a in range(8):
        @pl.when(zlo == a)
        def _(a=a):
            for s, to in sent_by(a):
                hand(s, to).wait_send()

    @pl.loop(0, 8)
    def _(s):
        across(s).wait_send()

    @pl.loop(0, 4)
    def _(k):
        for h in range(2):
            for j in range(3):
                send1(k, h, j).wait_send()
                send2(k, h, j).wait_send()
        send3(k).wait_send()


def shards(codes, scale_exp, delta):
    tokens, width = codes.shape
    total = float(tokens * lax.axis_size(TOK))
    padded = -(-tokens // 128) * 128
    dma = pltpu.SemaphoreType.DMA
    both = pl.pallas_call(
        functools.partial(kernel, total),
        out_shape=jax.ShapeDtypeStruct((64, 512), F32),
        in_specs=[pl.BlockSpec(memory_space=pl.ANY)] * 3,
        out_specs=pl.BlockSpec(memory_space=pltpu.VMEM),
        scratch_shapes=[
            pltpu.VMEM((padded, width), BF16),
            pltpu.VMEM((padded, width), BF16),
            pltpu.VMEM((8, 128), I32),
            pltpu.VMEM((2 * width, padded), BF16),
            pltpu.VMEM((512, padded), BF16),
            pltpu.VMEM((2, 4, 256, 128), F32),
            pltpu.VMEM((4, 2, 256, 128), F32),
            pltpu.VMEM((4, 2, 64, 128), F32),
            pltpu.VMEM((4, 2, 3, 272, 128), I16),
            pltpu.VMEM((4, 2, 3, 272, 128), I16),
            pltpu.VMEM((4, 2, 3, 80, 128), I16),
            pltpu.VMEM((4, 2, 3, 80, 128), I16),
            pltpu.VMEM((4, 80, 128), I16),
            pltpu.VMEM((4, 80, 128), I16),
            dma((4,)),
            dma((8, 8)),
            dma((8,)),
            dma((8, PARTS)),
            dma((8,)),
            dma((8,)),
            dma((4, 2, 3)),
            dma((4, 2, 3)),
            dma((4, 2, 3)),
            dma((4, 2, 3)),
            dma((4,)),
            dma((4,)),
            pltpu.SemaphoreType.REGULAR,
        ],
        compiler_params=pltpu.CompilerParams(
            collective_id=0, has_side_effects=True, vmem_limit_bytes=56 * 2**20
        ),
        cost_estimate=pl.CostEstimate(
            flops=2 * 2 * width * 512 * tokens, bytes_accessed=4 * tokens * width, transcendentals=0
        ),
    )(codes, scale_exp.reshape(width // 128, 128), delta)
    return both[:32] * (1.0 / total), both[32:] * (1.0 / total**0.5)


def solution(mesh):
    split = Mesh(mesh.devices.reshape(8, 2, 2, 4, 4), AXES)
    chan = ("zlo", "core")
    return jax.shard_map(
        shards,
        mesh=split,
        in_specs=(P(TOK, chan), P(chan), P(TOK, chan)),
        out_specs=(P((*chan, *TOK), None), P((*chan, *TOK), None)),
        check_vma=False,
    )
```

```python
import functools

import jax
import jax.numpy as jnp
from jax import lax
from jax.experimental import pallas as pl
from jax.experimental.pallas import tpu as pltpu
from jax.sharding import Mesh
from jax.sharding import PartitionSpec as P

WCOL = 32
AXES = ("zlo", "core", "zhi", "y", "x")
TOK = ("zhi", "y", "x")
MESH = pl.DeviceIdType.MESH
F32, BF16, I32, I16 = jnp.float32, jnp.bfloat16, jnp.int32, jnp.int16

DIRECT = {
    0: (4, 1),
    1: (5, 2, 0),
    2: (6, 1, 3),
    3: (6, 1, 4, 2),
    4: (1, 6, 3),
    5: (1, 4, 6),
    6: (2, 5, 7),
    7: (3, 6),
}
RELAY = {
    0: {},
    1: {0: (2,), 2: (0,), 3: (0,), 4: (0, 2), 5: (0, 2)},
    2: {1: (3,), 6: (0, 1, 3)},
    3: {2: (4,), 7: (0, 1, 2, 4)},
    4: {3: (5,), 5: (3,), 0: (7, 6, 3, 5)},
    5: {6: (4,), 1: (7, 4, 6)},
    6: {5: (7,), 7: (5,), 4: (5, 7), 3: (7,), 2: (5, 7)},
    7: {},
}
CHUNKS = {
    0: (0, 1, 2, 3),
    1: (0, 1, 2, 3),
    2: (1, 0, 2, 3),
    3: (1, 2, 0, 3),
    4: (2, 1, 3, 0),
    5: (2, 3, 1, 0),
    6: (3, 2, 1, 0),
    7: (3, 2, 1, 0),
}
PARTS = 5
TOP = 32000.0


def coded(value, groups):
    blocks = value.reshape(groups, 32, 128)
    largest = jnp.maximum(jnp.max(jnp.abs(blocks), axis=1), 2.0**-110)
    eighths = jnp.ceil(jnp.log2(largest) * 8.0)
    factor = jnp.exp2(eighths * -0.125) * TOP
    whole = jnp.round(blocks * factor[:, None, :]).astype(I32).astype(I16)
    if groups < 16:
        eighths = jnp.concatenate([eighths, jnp.zeros((16 - groups, 128), F32)], axis=0)
    return whole.reshape(groups * 32, 128), eighths.astype(I32).astype(I16)


def decoded(ref, at, groups):
    rows = groups * 32
    whole = ref[(*at, pl.ds(0, rows), slice(None))].astype(I32).astype(F32)
    eighths = ref[(*at, pl.ds(rows, 16), slice(None))].astype(I32).astype(F32)[:groups]
    factor = jnp.exp2(eighths * 0.125) * (1.0 / TOP)
    return (whole.reshape(groups, 32, 128) * factor[:, None, :]).reshape(rows, 128)


def kernel(total, codes, scale_exp, delta, out, xs, ds, scale, left, win, product, own1, own2,
           s1, r1, s2, r2, s3, r3, load_sem, wsend, wrecv, wpart, csend, crecv, q1s, q1r, q2s, q2r, q3s, q3r, go_sem):
    tokens, width = codes.shape
    padded = xs.shape[0]
    zlo, core, zhi, y, x = (lax.axis_index(a) for a in AXES)
    z = zhi * 8 + zlo

    def along(d):
        n = lax.rem(z + (d + 16), 16)
        return {"zhi": n // 8, "zlo": lax.rem(n, 8)}

    loads = [
        pltpu.make_async_copy(codes.at[:, pl.ds(0, 128)], xs.at[pl.ds(0, tokens), pl.ds(0, 128)], load_sem.at[0]),
        pltpu.make_async_copy(scale_exp, scale, load_sem.at[1]),
        pltpu.make_async_copy(codes.at[:, pl.ds(128, width - 128)], xs.at[pl.ds(0, tokens), pl.ds(128, width - 128)], load_sem.at[2]),
        pltpu.make_async_copy(delta, ds.at[pl.ds(0, tokens)], load_sem.at[3]),
    ]
    barrier = pltpu.get_barrier_semaphore()
    greet = [along(d) for d in (4, -4, 3, -3, 2, -2, 1, -1)]
    greet += [{a: lax.rem(lax.axis_index(a) + k, 4)} for a in ("x", "y") for k in (2, 1, 3)]
    greet += [{"core": 1 - core}]
    for who in greet:
        pl.semaphore_signal(barrier, inc=1, device_id=who, device_id_type=MESH)
    for c in loads:
        c.start()

    xs[pl.ds(tokens, padded - tokens), :] = jnp.zeros((padded - tokens, width), BF16)
    ds[pl.ds(tokens, padded - tokens), :] = jnp.zeros((padded - tokens, width), BF16)
    loads[0].wait()
    loads[1].wait()

    def factors(i):
        return jnp.exp2(scale[pl.ds(i, 1), :].astype(F32)).astype(BF16)

    my_rows = pl.ds(pl.multiple_of((zlo * 2 + core) * WCOL, WCOL), WCOL)
    win[my_rows, :] = (xs[:, pl.ds(0, 128)] * factors(0)).T[:WCOL]

    def place(i, stat, block):
        hi, row = i // 4, lax.rem(i, 4)
        for k in range(4):
            first = jnp.where(hi == 0, k * 4 + row, row * 4 + k)
            start = pl.multiple_of(hi * width + (first * 2 + stat) * 32, 32)
            left[pl.ds(start, 32), :] = block[k * 32 : (k + 1) * 32]

    pl.semaphore_wait(barrier, len(greet))
    pl.semaphore_signal(go_sem, inc=1, device_id=along(4), device_id_type=MESH)

    def block_rows(s, c):
        return pl.ds(pl.multiple_of((s * 2 + c) * WCOL, WCOL), WCOL)

    def hand(s, to, part=None, recv=None):
        size = padded // PARTS
        lanes = pl.ds(0, padded) if part is None else pl.ds(part * size, size)
        block = win.at[block_rows(s, core), lanes]
        return pltpu.make_async_remote_copy(
            src_ref=block, dst_ref=block, send_sem=wsend.at[s, to], recv_sem=wrecv.at[s] if recv is None else recv,
            device_id={"zlo": to}, device_id_type=MESH)

    def across(s):
        return pltpu.make_async_remote_copy(
            src_ref=win.at[block_rows(s, core)], dst_ref=win.at[block_rows(s, core)],
            send_sem=csend.at[s], recv_sem=crecv.at[s],
            device_id={"core": 1 - core}, device_id_type=MESH)

    def sent_by(a):
        return [(a, to) for to in DIRECT[a]] + [(s, to) for s, tos in RELAY[a].items() for to in tos]

    across(zlo).start()
    for a in range(8):
        @pl.when(zlo == a)
        def _(a=a):
            for part in range(PARTS):
                for to in DIRECT[a]:
                    if a in RELAY[to]:
                        hand(a, to, part, wpart.at[a, part]).start()
            for to in DIRECT[a]:
                if a not in RELAY[to]:
                    hand(a, to).start()
            pass

    loads[2].wait()
    loads[3].wait()

    @pl.loop(0, width // 128)
    def _(i):
        lanes = pl.ds(pl.multiple_of(i * 128, 128), 128)
        place(i, 0, (xs[:, lanes] * factors(i)).T)
        place(i, 1, ds[:, lanes].T)

    for a in range(8):
        @pl.when(zlo == a)
        def _(a=a):
            for s, tos in RELAY[a].items():
                for part in range(PARTS):
                    hand(s, a, part, wpart.at[s, part]).wait_recv()
                    for to in tos:
                        hand(s, to, part).start()
                across(s).start()

    def take(a, n):
        pair = (2 * CHUNKS[a][n], 2 * CHUNKS[a][n] + 1)
        for s in pair:
            if s != a and s not in RELAY[a]:
                hand(s, a).wait_recv()
                across(s).start()
        for s in pair:
            across(s).wait_recv()

    def chunk_of(k):
        q = jnp.int32(0)
        for a in range(8):
            for n in range(4):
                q = jnp.where((zlo == a) & (k == n), CHUNKS[a][n], q)
        return q

    halves = (1 - zhi, zhi)

    def hop(along_x, j):
        return {"x": jnp.where(along_x, lax.rem(x + j + 1, 4), x), "y": jnp.where(along_x, y, lax.rem(y + j + 1, 4))}

    def send1(k, h, j):
        return pltpu.make_async_remote_copy(
            src_ref=s1.at[k, h, j], dst_ref=r1.at[k, h, j], send_sem=q1s.at[k, h, j], recv_sem=q1r.at[k, h, j],
            device_id=hop(h == 0, j), device_id_type=MESH)

    def send2(k, h, j):
        return pltpu.make_async_remote_copy(
            src_ref=s2.at[k, h, j], dst_ref=r2.at[k, h, j], send_sem=q2s.at[k, h, j], recv_sem=q2r.at[k, h, j],
            device_id=hop(h == 1, j), device_id_type=MESH)

    def send3(k):
        return pltpu.make_async_remote_copy(
            src_ref=s3.at[k], dst_ref=r3.at[k], send_sem=q3s.at[k], recv_sem=q3r.at[k],
            device_id={"zhi": 1 - zhi}, device_id_type=MESH)

    def multiply(k):
        q = chunk_of(k)
        right = win[pl.ds(pl.multiple_of(q * 128, 128), 128), :]

        for n, h in enumerate(halves):
            me = jnp.where(h == 0, x, y)
            product[n] = lax.dot_general(
                left[pl.ds(pl.multiple_of(h * width, width), width), :], right,
                (((1,), (1,)), ((), ())), preferred_element_type=F32,
            ).reshape(4, width // 4, 128)

            @pl.loop(0, 3)
            def _(j, n=n, h=h, me=me):
                whole, eighths = coded(product[n, lax.rem(me + j + 1, 4)], 8)
                s1[k, h, j, pl.ds(0, 256), :] = whole
                s1[k, h, j, pl.ds(256, 16), :] = eighths
                send1(k, h, j).start()

            own1[k, h] = product[n, me]

    def second(k):
        for h in halves:
            for j in range(3):
                send1(k, h, j).wait_recv()
            me = jnp.where(h == 0, y, x)
            own1[k, h] = own1[k, h] + decoded(r1, (k, h, 0), 8) + decoded(r1, (k, h, 1), 8) + decoded(r1, (k, h, 2), 8)
            for j in range(3):
                t = lax.rem(me + j + 1, 4)
                whole, eighths = coded(own1[k, h, pl.ds(pl.multiple_of(t * 64, 64), 64), :], 2)
                s2[k, h, j, pl.ds(0, 64), :] = whole
                s2[k, h, j, pl.ds(64, 16), :] = eighths
                send2(k, h, j).start()
            own2[k, h] = own1[k, h, pl.ds(pl.multiple_of(me * 64, 64), 64), :]

    def third(k):
        for n, h in enumerate(halves):
            for j in range(3):
                send2(k, h, j).wait_recv()
            value = own2[k, h] + decoded(r2, (k, h, 0), 2) + decoded(r2, (k, h, 1), 2) + decoded(r2, (k, h, 2), 2)
            if n == 0:
                whole, eighths = coded(value, 2)
                s3[k, pl.ds(0, 64), :] = whole
                s3[k, pl.ds(64, 16), :] = eighths
                send3(k).start()
            else:
                own2[k, h] = value

    def last(k):
        send3(k).wait_recv()
        result = own2[k, zhi] + decoded(r3, (k,), 2)
        lanes = pl.ds(pl.multiple_of(chunk_of(k) * 128, 128), 128)
        out[:, lanes] = result

    @pl.loop(0, 4)
    def _(phase):
        for n in range(4):
            for a in range(8):
                @pl.when((phase == n) & (zlo == a))
                def _(n=n, a=a):
                    take(a, n)

        multiply(phase)

        @pl.when(phase >= 1)
        def _():
            second(phase - 1)

        @pl.when(phase == 2)
        def _():
            pl.semaphore_wait(go_sem, 1)

        @pl.when(phase >= 2)
        def _():
            third(phase - 2)

    second(3)
    third(2)
    third(3)

    @pl.loop(0, 4)
    def _(k):
        last(k)

    for a in range(8):
        @pl.when(zlo == a)
        def _(a=a):
            for s, to in sent_by(a):
                hand(s, to).wait_send()

    @pl.loop(0, 8)
    def _(s):
        across(s).wait_send()

    @pl.loop(0, 4)
    def _(k):
        for h in range(2):
            for j in range(3):
                send1(k, h, j).wait_send()
                send2(k, h, j).wait_send()
        send3(k).wait_send()


def shards(codes, scale_exp, delta):
    tokens, width = codes.shape
    total = float(tokens * lax.axis_size(TOK))
    padded = -(-tokens // 128) * 128
    dma = pltpu.SemaphoreType.DMA
    both = pl.pallas_call(
        functools.partial(kernel, total),
        out_shape=jax.ShapeDtypeStruct((64, 512), F32),
        in_specs=[pl.BlockSpec(memory_space=pl.ANY)] * 3,
        out_specs=pl.BlockSpec(memory_space=pltpu.VMEM),
        scratch_shapes=[
            pltpu.VMEM((padded, width), BF16),
            pltpu.VMEM((padded, width), BF16),
            pltpu.VMEM((8, 128), I32),
            pltpu.VMEM((2 * width, padded), BF16),
            pltpu.VMEM((512, padded), BF16),
            pltpu.VMEM((2, 4, 256, 128), F32),
            pltpu.VMEM((4, 2, 256, 128), F32),
            pltpu.VMEM((4, 2, 64, 128), F32),
            pltpu.VMEM((4, 2, 3, 272, 128), I16),
            pltpu.VMEM((4, 2, 3, 272, 128), I16),
            pltpu.VMEM((4, 2, 3, 80, 128), I16),
            pltpu.VMEM((4, 2, 3, 80, 128), I16),
            pltpu.VMEM((4, 80, 128), I16),
            pltpu.VMEM((4, 80, 128), I16),
            dma((4,)),
            dma((8, 8)),
            dma((8,)),
            dma((8, PARTS)),
            dma((8,)),
            dma((8,)),
            dma((4, 2, 3)),
            dma((4, 2, 3)),
            dma((4, 2, 3)),
            dma((4, 2, 3)),
            dma((4,)),
            dma((4,)),
            pltpu.SemaphoreType.REGULAR,
        ],
        compiler_params=pltpu.CompilerParams(
            collective_id=0, has_side_effects=True, vmem_limit_bytes=56 * 2**20
        ),
        cost_estimate=pl.CostEstimate(
            flops=2 * 2 * width * 512 * tokens, bytes_accessed=4 * tokens * width, transcendentals=0
        ),
    )(codes, scale_exp.reshape(width // 128, 128), delta)
    return both[:32] * (1.0 / total), both[32:] * (1.0 / total**0.5)


def solution(mesh):
    split = Mesh(mesh.devices.reshape(8, 2, 2, 4, 4), AXES)
    chan = ("zlo", "core")
    return jax.shard_map(
        shards,
        mesh=split,
        in_specs=(P(TOK, chan), P(chan), P(TOK, chan)),
        out_specs=(P((*chan, *TOK), None), P((*chan, *TOK), None)),
        check_vma=False,
    )
```
